256 devices in a mesh: expert: 64 (over z, x, core), dp: 4 (over y).
Axes of the slice: x: 4, y: 4, z: 8, core: 2. Of those that a mesh axis runs over, the one named last changes fastest.
Arguments:
- tokens: bfloat16 [2, 2048, 7168], P(None, ('expert', 'dp')), may hold values from -6 to 6
- expert_ids: int32 [2, 2048, 8], P(None, ('expert', 'dp')), may hold values from 0 to 63, all different within a row; in each aligned block of 8 rows (0 to 7, 8 to 15, ..., all dimensions but the last counted through in order) at most 2 rows name the same one
- gate_scores: float32 [2, 2048, 8], P(None, ('expert', 'dp')), may hold values from 0.05 to 0.5
- w_gate: bfloat16 [64, 7168, 1024], P('expert', 'dp'), may hold values from -0.0625 to 0.0625
- w_up: bfloat16 [64, 7168, 1024], P('expert', 'dp'), may hold values from -0.0625 to 0.0625
- w_down: bfloat16 [64, 1024, 7168], P('expert', None, 'dp'), may hold values from -0.1875 to 0.1875
Outputs:
- moe_out: bfloat16 [2, 2048, 7168], P(None, ('expert', 'dp'))
The draws below stay inside these ranges and needn't reach their ends.
Inputs may be any that keep to these rules, and one draw needn't show every extreme that they name: `expert_ids`: each row names 8 different values; in each step the rows of one device name one value at most 2 times, a bound that some block reaches.
All inputs are finite; a program needn't handle non-finite values.
Results may differ from the reference program's by a relative error of at most 0.0057.
Values may be sent and summed in bfloat16 or wider, within the bound.
No kernel may reach another device: no remote copies, remote signals or barrier semaphores. Data moves between devices by JAX's collectives and lax.ppermute only.
A program may use at most 128 MiB of HBM per device.

```python
import math
import jax
import jax.numpy as jnp
import numpy as np
from jax import lax

D = 7168
EH = 1024
TOPK = 8
TOK_DEV = 8
EXPERTS = 64
CAP = 2
TOKENS = 2048
N_EXPERT = 64
N_DP = 4


def block_levels(stream_key, shape, cuts, low, high):
    level, own = 1.0, jax.random.fold_in(stream_key, 6)
    for dim, shards_of in cuts:
        steps = jnp.exp(jax.random.uniform(jax.random.fold_in(own, dim), (shards_of,), jnp.float32, low / len(cuts), high / len(cuts)))
        level = level * jnp.repeat(steps, shape[dim] // shards_of).reshape([-1 if axis == dim else 1 for axis in range(len(shape))])
    return level


def shared_out(own_key, own, number, rows, count, top, reach, skew):
    order = jax.random.permutation(own_key, count)
    crowded, usual = load_shares(count, rows * top, reach, skew, True), load_shares(count, rows * top, reach, skew, False)
    places = jnp.arange(count)

    def named(tallies, turn):
        used = int((tallies > 0).sum())
        fixed = max(1, used // 4)
        moved = fixed + (places - fixed + turn * (used - fixed)) % max(1, count - fixed)
        return jnp.zeros((count,), jnp.int32).at[order[jnp.where(places < fixed, places, moved)]].set(jnp.asarray(tallies, jnp.int32))

    tallies = jnp.where(number % 4 == 0, named(crowded, number // 4), named(usual, number - number // 4 - 1))
    mixed = jax.random.permutation(jax.random.fold_in(own, 3), count)
    source_of, taker = mixed[0:count // 2 * 2:2], mixed[1:count // 2 * 2:2]
    margin = jnp.minimum(tallies[source_of] - 1, reach - tallies[taker]) // 2
    margin = jnp.where((source_of == order[0]) | (taker == order[0]) | (tallies[taker] == 0), 0, jnp.maximum(margin, 0))
    moved = jax.random.randint(jax.random.fold_in(own, 4), (count // 2,), 0, 1 << 20) % (margin + 1)
    tallies = tallies.at[source_of].add(-moved).at[taker].add(moved)
    items = jnp.searchsorted(jnp.cumsum(tallies), jnp.arange(rows * top), side="right").astype(jnp.int32)
    listing = items.reshape(top, rows).T
    listing = listing[jax.random.permutation(jax.random.fold_in(own, 1), rows)]
    turn = jax.random.randint(jax.random.fold_in(own, 2), (rows, 1), 0, top)
    return jnp.take_along_axis(listing, (jnp.arange(top)[None, :] + turn) % top, axis=1)


def load_shares(amount, total, most, lean, full):
    weights = [(1 << 20) // math.isqrt(rank ** lean) + 1 for rank in range(1, amount + 1)]
    largest = most if full else min(most, max(-(-total // amount), total * weights[0] // sum(weights)))
    least = 1 if total - largest >= amount - 1 else 0
    counts, rest = [largest] + [least] * (amount - 1), total - largest - least * (amount - 1)
    while rest > 0:
        candidates = [i for i in range(1, amount) if counts[i] < largest] or [i for i in range(1, amount) if counts[i] < most]
        mass, remaining = sum([weights[i] for i in candidates]), rest
        for i in candidates:
            extra = min(most - counts[i], max(1, remaining * weights[i] // mass), rest)
            counts[i] = counts[i] + extra
            rest = rest - extra
    return np.array(counts)


def gaussian(key, dims, scale, most, shards=(), dtype=jnp.bfloat16):
    level = block_levels(key, dims, shards, -0.22, 0.18) if shards else 1.0
    array = jax.random.normal(key, dims, jnp.float32) * scale * level
    return jnp.minimum(jnp.maximum(array, -most), most).astype(dtype)


def setup_inputs(seed: int = 0) -> dict:
    seeds = jax.random.split(jax.random.key(seed), 7)
    tokens = gaussian(seeds[0], (2, TOKENS, D), 1.0, 6.0, ((1, 256),))
    expert_ids_keys = jax.random.split(jax.random.fold_in(seeds[1], 1), 2 * TOKENS // TOK_DEV)
    expert_ids_turns = jax.random.permutation(jax.random.fold_in(seeds[1], 3), 2 * TOKENS // TOK_DEV)
    expert_ids = jax.vmap(lambda own, number: shared_out(jax.random.fold_in(seeds[1], 2), own, number, TOK_DEV, EXPERTS, TOPK, CAP, 2))(expert_ids_keys, expert_ids_turns).reshape((2, TOKENS, TOPK))
    gate_scores = jnp.clip(jnp.exp(math.log(0.5) - 2.3025851 * jax.random.uniform(seeds[2], (2, TOKENS, TOPK), jnp.float32) ** block_levels(seeds[2], (2, TOKENS, TOPK), ((1, 256),), -0.2, 0.2)), 0.05, 0.5)
    w_gate = gaussian(seeds[3], (EXPERTS, D, EH), D ** -0.5, 0.0625, ((0, 64), (1, 4)))
    w_up = gaussian(seeds[4], (EXPERTS, D, EH), D ** -0.5, 0.0625, ((0, 64), (1, 4)))
    w_down = gaussian(seeds[5], (EXPERTS, EH, D), EH ** -0.5, 0.1875, ((0, 64), (2, 4)))
    return {"tokens": tokens, "expert_ids": expert_ids, "gate_scores": gate_scores, "w_gate": w_gate, "w_up": w_up, "w_down": w_down}


def expert_rows(slot_rows, wg, wu, wd):
    gate = jnp.dot(slot_rows, wg, preferred_element_type=jnp.float32)
    upper = jnp.dot(slot_rows, wu, preferred_element_type=jnp.float32)
    hidden = (jax.nn.silu(gate) * upper).astype(jnp.bfloat16)
    return jnp.dot(hidden, wd, preferred_element_type=jnp.float32).astype(jnp.bfloat16)


def one_step(inputs, logical, scores, w_gate, w_up, w_down):
    most_rows = N_EXPERT * N_DP * CAP

    def per_expert(total, packet):
        number, wg, wu, wd = packet
        matched = logical == number
        weight_sum = jnp.sum(jnp.where(matched, scores, 0.0), axis=1)
        routed = jnp.any(matched, axis=1)
        where_rows = jnp.nonzero(routed, size=most_rows, fill_value=0)[0].astype(jnp.int32)
        valid = jnp.arange(most_rows) < jnp.sum(routed.astype(jnp.int32))
        slot_rows = inputs[where_rows]
        result = expert_rows(slot_rows, wg, wu, wd).astype(jnp.float32)
        factor = jnp.where(valid, weight_sum[where_rows], 0.0)
        total = total.at[where_rows].add(factor[:, None] * result)
        return total, None

    start = jnp.zeros((inputs.shape[0], inputs.shape[1]), jnp.float32)
    numbers = jnp.arange(EXPERTS).astype(jnp.int32)
    total, unused = lax.scan(per_expert, start, (numbers, w_gate, w_up, w_down))
    return total.astype(jnp.bfloat16)


def reference(tokens, expert_ids, gate_scores, w_gate, w_up, w_down):
    out_first = one_step(tokens[0], expert_ids[0], gate_scores[0], w_gate, w_up, w_down)
    out_second = one_step(tokens[1], expert_ids[1], gate_scores[1], w_gate, w_up, w_down)
    return jnp.stack([out_first, out_second])
```

```python
import jax
import jax.numpy as jnp
from jax import lax
from jax.sharding import PartitionSpec as P

AXES = ("expert", "dp")


def exchange(blocks):
    return lax.all_to_all(blocks, AXES, split_axis=0, concat_axis=0, tiled=True)


def shift(value, by):
    n = lax.axis_size("dp")
    return lax.ppermute(value, "dp", [(i, (i + by) % n) for i in range(n)])


def slot_masks(owners, n_owner, capacity):
    tok_rows = owners.shape[0]
    same = jnp.any(owners[:, :, None, None] == owners[None, None, :, :], axis=3)
    before = jnp.arange(tok_rows)[None, None, :] < jnp.arange(tok_rows)[:, None, None]
    position = jnp.sum((same & before).astype(jnp.int32), axis=2)
    experts = jnp.arange(n_owner, dtype=jnp.int32)[:, None, None, None]
    places = jnp.arange(capacity, dtype=jnp.int32)[None, :, None, None]
    return (owners[None, None] == experts) & (position[None, None] == places)


def dispatch(inputs, masks):
    n_owner, capacity, tok_rows, _ = masks.shape
    n_rows = lax.axis_size("dp")
    share = inputs.shape[1] // n_rows
    selector = jnp.any(masks, axis=3).astype(jnp.bfloat16).reshape(n_owner * capacity, tok_rows)
    packed = jnp.dot(selector, inputs, preferred_element_type=jnp.float32).astype(jnp.bfloat16)
    blocks = packed.reshape(n_owner, capacity, n_rows, share).transpose(0, 2, 1, 3)
    return exchange(blocks.reshape(n_owner * n_rows, capacity, share)).reshape(-1, share)


def hidden_rows(slot_rows, wg, wu):
    n = lax.axis_size("dp")
    me = lax.axis_index("dp")
    block = slot_rows.shape[0] // n

    def rows_of(offset):
        return lax.dynamic_slice_in_dim(slot_rows, lax.rem(me + offset, n) * block, block, axis=0)

    def project(rows, weight):
        return jnp.dot(rows, weight, preferred_element_type=jnp.float32)

    far = rows_of(2)
    far_gate = shift(project(far, wg).astype(jnp.bfloat16), 1)
    far_up = shift(project(far, wu).astype(jnp.bfloat16), -1)
    near = jnp.concatenate([rows_of(1), rows_of(3), rows_of(0)], axis=0)
    gate, up = project(near, wg), project(near, wu)
    gate_next = (gate[:block] + far_gate.astype(jnp.float32)).astype(jnp.bfloat16)
    up_next = up[:block].astype(jnp.bfloat16)
    gate_prev = gate[block:2 * block].astype(jnp.bfloat16)
    up_prev = (up[block:2 * block] + far_up.astype(jnp.float32)).astype(jnp.bfloat16)
    gate_a, up_a = shift(gate_next, 1), shift(up_next, 1)
    gate_b, up_b = shift(gate_prev, -1), shift(up_prev, -1)
    gate_sum = gate[2 * block:] + gate_a.astype(jnp.float32) + gate_b.astype(jnp.float32)
    up_sum = up[2 * block:] + up_a.astype(jnp.float32) + up_b.astype(jnp.float32)
    own = (jax.nn.silu(gate_sum) * up_sum).astype(jnp.bfloat16)
    half = own.shape[1] // 2
    prev, following = shift(own, 1), shift(own, -1)
    opposite = jnp.concatenate([shift(prev[:, :half], 1), shift(following[:, half:], -1)], axis=1)
    hidden = jnp.zeros((n * block, own.shape[1]), jnp.bfloat16)
    for offset, piece in ((0, own), (1, following), (2, opposite), (3, prev)):
        hidden = lax.dynamic_update_slice_in_dim(hidden, piece, lax.rem(me + offset, n) * block, axis=0)
    return hidden


def expert_step(slot_rows, wg, wu, wd):
    hidden = hidden_rows(slot_rows, wg, wu)
    return jnp.dot(hidden, wd, preferred_element_type=jnp.float32).astype(jnp.bfloat16)


def send_back(expert_out, capacity):
    return exchange(expert_out.reshape(-1, capacity, expert_out.shape[1]))


def combine(returned, masks, scores):
    n_owner, capacity, tok_rows, _ = masks.shape
    n_rows = lax.axis_size("dp")
    share = returned.shape[-1]
    rows = returned.reshape(n_owner, n_rows, capacity, share).transpose(0, 2, 1, 3)
    rows = rows.reshape(n_owner * capacity, n_rows * share)
    factor = jnp.sum(jnp.where(masks, scores[None, None], 0.0), axis=3).reshape(n_owner * capacity, tok_rows)
    high = lax.reduce_precision(factor, 8, 7)
    middle = lax.reduce_precision(factor - high, 8, 7)
    low = factor - high - middle
    parts = jnp.concatenate([high, middle, low], axis=1).astype(jnp.bfloat16)
    sums = lax.dot_general(parts, rows, (((0,), (0,)), ((), ())), preferred_element_type=jnp.float32)
    total = sums[:tok_rows] + sums[tok_rows:2 * tok_rows] + sums[2 * tok_rows:]
    return total.astype(jnp.bfloat16)


def on_device(tokens, expert_ids, gate_scores, w_gate, w_up, w_down):
    steps, tok_rows, top_count = expert_ids.shape
    n_owner = lax.axis_size("expert")
    capacity = max(2, min(tok_rows, 2 * tok_rows * top_count // n_owner))
    masks = [slot_masks(expert_ids[i], n_owner, capacity) for i in range(steps)]
    slots = [dispatch(tokens[i], masks[i]) for i in range(steps)]
    outs = []
    for i in range(steps):
        result = expert_step(slots[i], w_gate[0], w_up[0], w_down[0])
        outs.append(combine(send_back(result, capacity), masks[i], gate_scores[i]))
    return jnp.stack(outs)


def solution(mesh):
    return jax.shard_map(
        on_device,
        mesh=mesh,
        in_specs=(
            P(None, AXES, None),
            P(None, AXES, None),
            P(None, AXES, None),
            P("expert", "dp", None),
            P("expert", "dp", None),
            P("expert", None, "dp"),
        ),
        out_specs=P(None, AXES, None),
        check_vma=False,
    )
```

```python
import jax
import jax.numpy as jnp
from jax import lax
from jax.sharding import Mesh, PartitionSpec as P

AXES = ("z", "x", "c", "y")
EXTRA = 128


def exchange(blocks, axes):
    return lax.all_to_all(blocks, axes, split_axis=0, concat_axis=0, tiled=True)


def shift(value, axis, by):
    n = lax.axis_size(axis)
    return lax.ppermute(value, axis, [(i, (i + by) % n) for i in range(n)])


def ring_gather(rows, axis):
    n = lax.axis_size(axis)
    blocks = {0: rows}
    upward = downward = rows
    for hop in range(1, (n + 1) // 2):
        upward, downward = shift(upward, axis, 1), shift(downward, axis, -1)
        blocks[n - hop], blocks[hop] = upward, downward
    half = -(-rows.shape[1] // 256) * 128
    blocks[n // 2] = jnp.concatenate(
        [shift(upward[:, :half], axis, 1), shift(downward[:, half:], axis, -1)], axis=1
    )
    return [blocks[i] for i in range(n)]


def slot_codes(owners, capacity):
    tok_rows = owners.shape[0]
    same = jnp.any(owners[:, :, None, None] == owners[None, None, :, :], axis=3)
    before = jnp.arange(tok_rows)[None, None, :] < jnp.arange(tok_rows)[:, None, None]
    return owners * capacity + jnp.sum((same & before).astype(jnp.int32), axis=2)


def three_parts(values):
    high = lax.reduce_precision(values, 8, 7)
    middle = lax.reduce_precision(values - high, 8, 7)
    return high, middle, values - high - middle


def with_extra(inputs, owners, scores, capacity):
    n_rows = lax.axis_size("y")
    tok_rows, width = inputs.shape
    shares = inputs.reshape(tok_rows, n_rows, width // n_rows).transpose(1, 0, 2)
    columns = [slot_codes(owners, capacity).astype(jnp.float32), *three_parts(scores)]
    extra = jnp.concatenate(columns, axis=1).astype(jnp.bfloat16)
    extra = jnp.pad(extra, ((0, 0), (0, EXTRA - extra.shape[1])))
    return jnp.concatenate(
        [shares, jnp.broadcast_to(extra[None], (n_rows, tok_rows, EXTRA))], axis=2
    )


def hit_sums(codes, groups, columns, values):
    keys = codes + groups[:, None]
    total = 0.0
    for k in range(codes.shape[1]):
        total = total + jnp.where(keys[:, k : k + 1] == columns[None, :], values[:, k : k + 1], 0.0)
    return total


def project(rows, weight):
    return jnp.dot(rows, weight, preferred_element_type=jnp.float32)


def contract_rows(left, right):
    return lax.dot_general(left, right, (((0,), (0,)), ((), ())), preferred_element_type=jnp.float32)


def hidden_rows(slot_rows, wg, wu):
    n = lax.axis_size("y")
    me = lax.axis_index("y")
    block = slot_rows.shape[0] // n

    def rows_of(offset):
        return lax.dynamic_slice_in_dim(slot_rows, lax.rem(me + offset, n) * block, block, axis=0)

    far = rows_of(2)
    far_gate = shift(project(far, wg).astype(jnp.bfloat16), "y", 1)
    far_up = shift(project(far, wu).astype(jnp.bfloat16), "y", -1)
    near = jnp.concatenate([rows_of(1), rows_of(3), rows_of(0)], axis=0)
    gate, up = project(near, wg), project(near, wu)
    gate_next = (gate[:block] + far_gate.astype(jnp.float32)).astype(jnp.bfloat16)
    up_next = up[:block].astype(jnp.bfloat16)
    gate_prev = gate[block : 2 * block].astype(jnp.bfloat16)
    up_prev = (up[block : 2 * block] + far_up.astype(jnp.float32)).astype(jnp.bfloat16)
    gate_a, up_a = shift(gate_next, "y", 1), shift(up_next, "y", 1)
    gate_b, up_b = shift(gate_prev, "y", -1), shift(up_prev, "y", -1)
    gate_sum = gate[2 * block :] + gate_a.astype(jnp.float32) + gate_b.astype(jnp.float32)
    up_sum = up[2 * block :] + up_a.astype(jnp.float32) + up_b.astype(jnp.float32)
    own = (jax.nn.silu(gate_sum) * up_sum).astype(jnp.bfloat16)
    pieces = ring_gather(own, "y")
    hidden = jnp.zeros((n * block, own.shape[1]), jnp.bfloat16)
    for offset, piece in enumerate(pieces):
        hidden = lax.dynamic_update_slice_in_dim(hidden, piece, lax.rem(me + offset, n) * block, axis=0)
    return hidden


def on_device(tokens, expert_ids, gate_scores, w_gate, w_up, w_down):
    steps, tok_rows, top_count = expert_ids.shape
    n_z, n_rows = lax.axis_size("z"), lax.axis_size("y")
    n_plane = lax.axis_size("x") * lax.axis_size("c")
    n_owner = n_z * n_plane
    share = tokens.shape[2] // n_rows
    capacity = max(2, min(tok_rows, 2 * tok_rows * top_count // n_owner))
    plane = lax.axis_index("z")
    span = n_owner * capacity
    sources = n_z * n_rows

    packed = jnp.concatenate(
        [with_extra(tokens[i], expert_ids[i], gate_scores[i], capacity) for i in range(steps)], axis=1
    )
    local = exchange(packed, "y").reshape(n_rows, steps, tok_rows, share + EXTRA)
    local = local.transpose(1, 0, 2, 3).reshape(steps * n_rows * tok_rows, share + EXTRA)
    blocks = ring_gather(local, "z")

    slot = jnp.arange(n_plane * sources * capacity, dtype=jnp.int32)
    peer, source = slot // (sources * capacity), slot // capacity % sources
    columns = (plane * n_plane + peer) * capacity + slot % capacity + span * source
    tok = jnp.arange(sources * tok_rows, dtype=jnp.int32)
    groups = tok // tok_rows * span
    rows_z = n_rows * tok_rows
    groups_z = (lax.rem(tok // rows_z - plane + n_z, n_z) * n_rows + tok // tok_rows % n_rows) * span

    slots, weights = [], []
    for i in range(steps):
        part = [b[i * rows_z : (i + 1) * rows_z] for b in blocks]
        gathered = jnp.concatenate(part, axis=0)
        extra = gathered[:, share:].astype(jnp.float32)
        codes = extra[:, :top_count].astype(jnp.int32)
        chosen = hit_sums(codes, groups, columns, jnp.ones(codes.shape, jnp.float32))
        rows = contract_rows(chosen.astype(jnp.bfloat16), gathered[:, :share]).astype(jnp.bfloat16)
        received = exchange(rows.reshape(n_plane, -1, share), ("x", "c"))
        slots.append(received.reshape(-1, share))
        ordered = lax.dynamic_slice_in_dim(
            jnp.concatenate([extra, extra], axis=0), lax.rem(n_z - plane, n_z) * rows_z, tok.shape[0], axis=0
        )
        codes = ordered[:, :top_count].astype(jnp.int32)
        scores = sum(ordered[:, j * top_count : (j + 1) * top_count] for j in (1, 2, 3))
        factor = hit_sums(codes, groups_z, columns, scores)
        weights.append(jnp.concatenate(three_parts(factor), axis=0).astype(jnp.bfloat16))

    outs = []
    for i in range(steps):
        hidden = hidden_rows(slots[i], w_gate[0], w_up[0])
        result = project(hidden, w_down[0]).astype(jnp.bfloat16)
        returned = exchange(result.reshape(n_plane, -1, share), ("x", "c")).reshape(-1, share)
        sums = project(weights[i], returned).reshape(3, sources, tok_rows, share)
        partial = (sums[0] + sums[1] + sums[2]).astype(jnp.bfloat16)
        collected = exchange(partial, ("z", "y")).reshape(n_z, n_rows, tok_rows, share)
        total = jnp.sum(collected.astype(jnp.float32), axis=0).astype(jnp.bfloat16)
        outs.append(total.transpose(1, 0, 2).reshape(tok_rows, n_rows * share))
    return jnp.stack(outs)


def solution(mesh):
    split = Mesh(mesh.devices.reshape(8, 4, 2, 4), AXES)
    expert = ("z", "x", "c")
    return jax.shard_map(
        on_device,
        mesh=split,
        in_specs=(
            P(None, AXES, None),
            P(None, AXES, None),
            P(None, AXES, None),
            P(expert, "y", None),
            P(expert, "y", None),
            P(expert, None, "y"),
        ),
        out_specs=P(None, AXES, None),
        check_vma=False,
    )
```

```python
import jax
import jax.numpy as jnp
from jax import lax
from jax.sharding import Mesh, PartitionSpec as P

AXES = ("z", "x", "c", "y")
EXTRA = 128


def exchange(blocks, axes):
    return lax.all_to_all(blocks, axes, split_axis=0, concat_axis=0, tiled=True)


def shift(value, axis, by):
    n = lax.axis_size(axis)
    return lax.ppermute(value, axis, [(i, (i + by) % n) for i in range(n)])


def ring_gather(rows, axis):
    n = lax.axis_size(axis)
    blocks = {0: rows}
    upward = downward = rows
    for hop in range(1, (n + 1) // 2):
        upward, downward = shift(upward, axis, 1), shift(downward, axis, -1)
        blocks[n - hop], blocks[hop] = upward, downward
    half = -(-rows.shape[1] // 256) * 128
    blocks[n // 2] = jnp.concatenate(
        [shift(upward[:, :half], axis, 1), shift(downward[:, half:], axis, -1)], axis=1
    )
    return [blocks[i] for i in range(n)]


SEND_RELATIVE = (True, True)
BACK_RELATIVE = (True, True)
PEERS = ((0, 0), (0, 1), (2, 0), (2, 1), (1, 0), (1, 1), (3, 0), (3, 1))


def plane_shifts(blocks, sign):
    n_x, n_c = lax.axis_size("x"), lax.axis_size("c")
    moved = []
    for block, (step_x, step_c) in zip(blocks, PEERS):
        if step_x or step_c:
            pairs = [
                (x * n_c + c, (x + sign * step_x) % n_x * n_c + (c + step_c) % n_c)
                for x in range(n_x)
                for c in range(n_c)
            ]
            block = lax.ppermute(block, ("x", "c"), pairs)
        moved.append(block)
    return jnp.concatenate(moved, axis=0)


def plane_places(sign):
    n_x, n_c = lax.axis_size("x"), lax.axis_size("c")
    x, c = lax.axis_index("x"), lax.axis_index("c")
    return [
        lax.rem(x + sign * step_x + n_x, n_x) * n_c + lax.rem(c + step_c, n_c) for step_x, step_c in PEERS
    ]


def plane_exchange(rows, relative):
    blocks = rows.reshape(len(PEERS), -1, rows.shape[1])
    if relative:
        return plane_shifts([blocks[j] for j in range(len(PEERS))], 1)
    return exchange(blocks, ("x", "c")).reshape(rows.shape)


def plane_return(rows, came_relative, relative):
    if not relative:
        return plane_exchange(rows, False)
    size = rows.shape[0] // len(PEERS)
    if came_relative:
        starts = [j * size for j in range(len(PEERS))]
    else:
        starts = [place * size for place in plane_places(-1)]
    return plane_shifts([lax.dynamic_slice_in_dim(rows, start, size, axis=0) for start in starts], -1)


def slot_codes(owners, capacity):
    tok_rows = owners.shape[0]
    same = jnp.any(owners[:, :, None, None] == owners[None, None, :, :], axis=3)
    before = jnp.arange(tok_rows)[None, None, :] < jnp.arange(tok_rows)[:, None, None]
    return owners * capacity + jnp.sum((same & before).astype(jnp.int32), axis=2)


def three_parts(values):
    high = lax.reduce_precision(values, 8, 7)
    middle = lax.reduce_precision(values - high, 8, 7)
    return high, middle, values - high - middle


def with_extra(inputs, owners, scores, capacity):
    n_rows = lax.axis_size("y")
    tok_rows, width = inputs.shape
    shares = inputs.reshape(tok_rows, n_rows, width // n_rows).transpose(1, 0, 2)
    columns = [slot_codes(owners, capacity).astype(jnp.float32), *three_parts(scores)]
    extra = jnp.concatenate(columns, axis=1).astype(jnp.bfloat16)
    extra = jnp.pad(extra, ((0, 0), (0, EXTRA - extra.shape[1])))
    return jnp.concatenate(
        [shares, jnp.broadcast_to(extra[None], (n_rows, tok_rows, EXTRA))], axis=2
    )


def hit_sums(codes, groups, columns, values):
    keys = codes + groups[:, None]
    total = 0.0
    for k in range(codes.shape[1]):
        total = total + jnp.where(keys[:, k : k + 1] == columns[None, :], values[:, k : k + 1], 0.0)
    return total


def project(rows, weight):
    return jnp.dot(rows, weight, preferred_element_type=jnp.float32)


def contract_rows(left, right):
    return lax.dot_general(left, right, (((0,), (0,)), ((), ())), preferred_element_type=jnp.float32)


def block_rows(rows, offset):
    n = lax.axis_size("y")
    block = rows.shape[0] // n
    return lax.dynamic_slice_in_dim(rows, lax.rem(lax.axis_index("y") + offset, n) * block, block, axis=0)


def first_stage(slot_rows, wg, wu):
    block = slot_rows.shape[0] // lax.axis_size("y")
    far = block_rows(slot_rows, 2)
    far_gate = shift(project(far, wg).astype(jnp.bfloat16), "y", 1)
    far_up = shift(project(far, wu).astype(jnp.bfloat16), "y", -1)
    near = jnp.concatenate([block_rows(slot_rows, 1), block_rows(slot_rows, 3), block_rows(slot_rows, 0)], axis=0)
    gate, up = project(near, wg), project(near, wu)
    gate_next = (gate[:block] + far_gate.astype(jnp.float32)).astype(jnp.bfloat16)
    up_next = up[:block].astype(jnp.bfloat16)
    gate_prev = gate[block : 2 * block].astype(jnp.bfloat16)
    up_prev = (up[block : 2 * block] + far_up.astype(jnp.float32)).astype(jnp.bfloat16)
    return (gate_next, up_prev), (up_next, gate_prev, gate[2 * block :], up[2 * block :])


def second_stage(summed, rest):
    (gate_next, up_prev), (up_next, gate_prev, gate, up) = summed, rest
    for value, by in ((gate_next, 1), (gate_prev, -1)):
        gate = gate + shift(value, "y", by).astype(jnp.float32)
    for value, by in ((up_next, 1), (up_prev, -1)):
        up = up + shift(value, "y", by).astype(jnp.float32)
    return gate, up


def joined(pieces):
    n, block = len(pieces), pieces[0].shape[0]
    rows = jnp.zeros((n * block, pieces[0].shape[1]), pieces[0].dtype)
    for offset, piece in enumerate(pieces):
        start = lax.rem(lax.axis_index("y") + offset, n) * block
        rows = lax.dynamic_update_slice_in_dim(rows, piece, start, axis=0)
    return rows


def on_device(tokens, expert_ids, gate_scores, w_gate, w_up, w_down):
    steps, tok_rows, top_count = expert_ids.shape
    n_z, n_rows = lax.axis_size("z"), lax.axis_size("y")
    n_plane = lax.axis_size("x") * lax.axis_size("c")
    n_owner = n_z * n_plane
    share = tokens.shape[2] // n_rows
    capacity = max(2, min(tok_rows, 2 * tok_rows * top_count // n_owner))
    plane = lax.axis_index("z")
    span = n_owner * capacity
    sources = n_z * n_rows

    packed = jnp.concatenate(
        [with_extra(tokens[i], expert_ids[i], gate_scores[i], capacity) for i in range(steps)], axis=1
    )
    local = exchange(packed, "y").reshape(n_rows, steps, tok_rows, share + EXTRA)
    local = local.transpose(1, 0, 2, 3).reshape(steps * n_rows * tok_rows, share + EXTRA)
    rows_z = n_rows * tok_rows
    blocks = [ring_gather(local[i * rows_z : (i + 1) * rows_z], "z") for i in range(steps)]

    slot = jnp.arange(n_plane * sources * capacity, dtype=jnp.int32)
    index, source = slot // (sources * capacity), slot // capacity % sources
    size = sources * capacity
    relative = jnp.concatenate([jnp.full((size,), place, jnp.int32) for place in plane_places(1)])
    within = plane * n_plane * capacity + slot % capacity + span * source
    columns = {False: within + index * capacity, True: within + relative * capacity}
    tok = jnp.arange(sources * tok_rows, dtype=jnp.int32)
    groups = tok // tok_rows * span
    groups_z = (lax.rem(tok // rows_z - plane + n_z, n_z) * n_rows + tok // tok_rows % n_rows) * span

    slots, weights = [], []
    for i in range(steps):
        gathered = jnp.concatenate(blocks[i], axis=0)
        extra = gathered[:, share:].astype(jnp.float32)
        codes = extra[:, :top_count].astype(jnp.int32)
        chosen = hit_sums(codes, groups, columns[SEND_RELATIVE[i]], jnp.ones(codes.shape, jnp.float32))
        rows = contract_rows(chosen.astype(jnp.bfloat16), gathered[:, :share]).astype(jnp.bfloat16)
        slots.append(plane_exchange(rows, SEND_RELATIVE[i]))
        ordered = lax.dynamic_slice_in_dim(
            jnp.concatenate([extra, extra], axis=0), lax.rem(n_z - plane, n_z) * rows_z, tok.shape[0], axis=0
        )
        codes = ordered[:, :top_count].astype(jnp.int32)
        scores = sum(ordered[:, j * top_count : (j + 1) * top_count] for j in (1, 2, 3))
        factor = hit_sums(codes, groups_z, columns[BACK_RELATIVE[i]], scores)
        weights.append(jnp.concatenate(three_parts(factor), axis=0).astype(jnp.bfloat16))

    outs = []
    for i in range(steps):
        gate, up = second_stage(*first_stage(slots[i], w_gate[0], w_up[0]))
        own = (jax.nn.silu(gate) * up).astype(jnp.bfloat16)
        hidden = joined(ring_gather(own, "y"))
        result = project(hidden, w_down[0]).astype(jnp.bfloat16)
        returned = plane_return(result, SEND_RELATIVE[i], BACK_RELATIVE[i])
        sums = project(weights[i], returned).reshape(3, sources, tok_rows, share)
        partial = (sums[0] + sums[1] + sums[2]).astype(jnp.bfloat16)
        collected = exchange(partial, ("z", "y")).reshape(n_z, n_rows, tok_rows, share)
        total = jnp.sum(collected.astype(jnp.float32), axis=0).astype(jnp.bfloat16)
        outs.append(total.transpose(1, 0, 2).reshape(tok_rows, n_rows * share))
    return jnp.stack(outs)


def solution(mesh):
    split = Mesh(mesh.devices.reshape(8, 4, 2, 4), AXES)
    expert = ("z", "x", "c")
    return jax.shard_map(
        on_device,
        mesh=split,
        in_specs=(
            P(None, AXES, None),
            P(None, AXES, None),
            P(None, AXES, None),
            P(expert, "y", None),
            P(expert, "y", None),
            P(expert, None, "y"),
        ),
        out_specs=P(None, AXES, None),
        check_vma=False,
    )
```

```python
import jax
import jax.numpy as jnp
from jax import lax
from jax.sharding import Mesh, PartitionSpec as P

AXES = ("z", "x", "c", "y")
EXTRA = 128


def phase(*values):
    return lax.optimization_barrier(values)


def exchange(blocks, axes):
    return lax.all_to_all(blocks, axes, split_axis=0, concat_axis=0, tiled=True)


def shift(value, axis, by):
    n = lax.axis_size(axis)
    return lax.ppermute(value, axis, [(i, (i + by) % n) for i in range(n)])


def ring_gather(rows, axis):
    n = lax.axis_size(axis)
    blocks = {0: rows}
    upward = downward = rows
    for hop in range(1, (n + 1) // 2):
        upward, downward = shift(upward, axis, 1), shift(downward, axis, -1)
        blocks[n - hop], blocks[hop] = upward, downward
    half = -(-rows.shape[1] // 256) * 128
    blocks[n // 2] = jnp.concatenate(
        [shift(upward[:, :half], axis, 1), shift(downward[:, half:], axis, -1)], axis=1
    )
    return [blocks[i] for i in range(n)]


SEND_RELATIVE = (True, False)
BACK_RELATIVE = (False, True)
PEERS = ((0, 0), (0, 1), (2, 0), (2, 1), (1, 0), (1, 1), (3, 0), (3, 1))


def plane_shifts(blocks, sign):
    n_x, n_c = lax.axis_size("x"), lax.axis_size("c")
    moved = []
    for block, (step_x, step_c) in zip(blocks, PEERS):
        if step_x or step_c:
            pairs = [
                (x * n_c + c, (x + sign * step_x) % n_x * n_c + (c + step_c) % n_c)
                for x in range(n_x)
                for c in range(n_c)
            ]
            block = lax.ppermute(block, ("x", "c"), pairs)
        moved.append(block)
    return moved


def plane_places(sign):
    n_x, n_c = lax.axis_size("x"), lax.axis_size("c")
    x, c = lax.axis_index("x"), lax.axis_index("c")
    return [
        lax.rem(x + sign * step_x + n_x, n_x) * n_c + lax.rem(c + step_c, n_c) for step_x, step_c in PEERS
    ]


def plane_send(rows, relative):
    size = rows.shape[0] // len(PEERS)
    if not relative:
        return exchange(rows.reshape(len(PEERS), size, -1), ("x", "c")).reshape(rows.shape)
    moved = plane_shifts([rows[j * size : (j + 1) * size] for j in range(len(PEERS))], 1)
    arrived = jnp.zeros(rows.shape, rows.dtype)
    for block, place in zip(moved, plane_places(-1)):
        arrived = lax.dynamic_update_slice_in_dim(arrived, block, place * size, axis=0)
    return arrived


def plane_return(rows, relative):
    size = rows.shape[0] // len(PEERS)
    if not relative:
        return exchange(rows.reshape(len(PEERS), size, -1), ("x", "c")).reshape(rows.shape)
    blocks = [lax.dynamic_slice_in_dim(rows, place * size, size, axis=0) for place in plane_places(-1)]
    return plane_shifts(blocks, -1)


def slot_codes(owners, capacity):
    tok_rows = owners.shape[0]
    same = jnp.any(owners[:, :, None, None] == owners[None, None, :, :], axis=3)
    before = jnp.arange(tok_rows)[None, None, :] < jnp.arange(tok_rows)[:, None, None]
    return owners * capacity + jnp.sum((same & before).astype(jnp.int32), axis=2)


def three_parts(values):
    high = lax.reduce_precision(values, 8, 7)
    middle = lax.reduce_precision(values - high, 8, 7)
    return high, middle, values - high - middle


def with_extra(inputs, owners, scores, capacity):
    n_rows = lax.axis_size("y")
    tok_rows, width = inputs.shape
    shares = inputs.reshape(tok_rows, n_rows, width // n_rows).transpose(1, 0, 2)
    columns = [slot_codes(owners, capacity).astype(jnp.float32), *three_parts(scores)]
    extra = jnp.concatenate(columns, axis=1).astype(jnp.bfloat16)
    extra = jnp.pad(extra, ((0, 0), (0, EXTRA - extra.shape[1])))
    return jnp.concatenate(
        [shares, jnp.broadcast_to(extra[None], (n_rows, tok_rows, EXTRA))], axis=2
    )


def hit_sums(codes, groups, columns, values):
    keys = codes + groups[:, None]
    total = 0.0
    for k in range(codes.shape[1]):
        total = total + jnp.where(keys[:, k : k + 1] == columns[None, :], values[:, k : k + 1], 0.0)
    return total


def project(rows, weight):
    return jnp.dot(rows, weight, preferred_element_type=jnp.float32)


def contract_rows(left, right):
    return lax.dot_general(left, right, (((0,), (0,)), ((), ())), preferred_element_type=jnp.float32)


def block_rows(rows, offset):
    n = lax.axis_size("y")
    block = rows.shape[0] // n
    return lax.dynamic_slice_in_dim(rows, lax.rem(lax.axis_index("y") + offset, n) * block, block, axis=0)


def first_stage(slot_rows, wg, wu, after):
    block = slot_rows.shape[0] // lax.axis_size("y")
    far = block_rows(slot_rows, 2)
    far_gate, far_up = project(far, wg).astype(jnp.bfloat16), project(far, wu).astype(jnp.bfloat16)
    if after:
        far_gate, far_up = phase(far_gate, far_up, *after)[:2]
    far_gate, far_up = shift(far_gate, "y", 1), shift(far_up, "y", -1)
    near = jnp.concatenate([block_rows(slot_rows, 1), block_rows(slot_rows, 3), block_rows(slot_rows, 0)], axis=0)
    gate, up = project(near, wg), project(near, wu)
    gate_next = (gate[:block] + far_gate.astype(jnp.float32)).astype(jnp.bfloat16)
    up_next = up[:block].astype(jnp.bfloat16)
    gate_prev = gate[block : 2 * block].astype(jnp.bfloat16)
    up_prev = (up[block : 2 * block] + far_up.astype(jnp.float32)).astype(jnp.bfloat16)
    return (gate_next, up_prev), (up_next, gate_prev, gate[2 * block :], up[2 * block :])


def second_stage(summed, rest):
    (gate_next, up_prev), (up_next, gate_prev, gate, up) = summed, rest
    for value, by in ((gate_next, 1), (gate_prev, -1)):
        gate = gate + shift(value, "y", by).astype(jnp.float32)
    for value, by in ((up_next, 1), (up_prev, -1)):
        up = up + shift(value, "y", by).astype(jnp.float32)
    return gate, up


def joined(pieces):
    n, block = len(pieces), pieces[0].shape[0]
    rows = jnp.zeros((n * block, pieces[0].shape[1]), pieces[0].dtype)
    for offset, piece in enumerate(pieces):
        start = lax.rem(lax.axis_index("y") + offset, n) * block
        rows = lax.dynamic_update_slice_in_dim(rows, piece, start, axis=0)
    return rows


def on_device(tokens, expert_ids, gate_scores, w_gate, w_up, w_down):
    steps, tok_rows, top_count = expert_ids.shape
    n_z, n_rows = lax.axis_size("z"), lax.axis_size("y")
    n_plane = lax.axis_size("x") * lax.axis_size("c")
    n_owner = n_z * n_plane
    share = tokens.shape[2] // n_rows
    capacity = max(2, min(tok_rows, 2 * tok_rows * top_count // n_owner))
    plane = lax.axis_index("z")
    span = n_owner * capacity
    sources = n_z * n_rows

    slot = jnp.arange(n_plane * sources * capacity, dtype=jnp.int32)
    index, source = slot // (sources * capacity), slot // capacity % sources
    size = sources * capacity
    relative = jnp.concatenate([jnp.full((size,), place, jnp.int32) for place in plane_places(1)])
    within = plane * n_plane * capacity + slot % capacity + span * source
    columns = {False: within + index * capacity, True: within + relative * capacity}
    tok = jnp.arange(sources * tok_rows, dtype=jnp.int32)
    groups = tok // tok_rows * span

    def arrive(i):
        packed = with_extra(tokens[i], expert_ids[i], gate_scores[i], capacity)
        return exchange(jnp.tile(packed, (n_z, 1, 1)), ("z", "y")).reshape(tok.shape[0], share + EXTRA)

    def pick(i, gathered):
        codes = gathered[:, share : share + top_count].astype(jnp.int32)
        chosen = hit_sums(codes, groups, columns[SEND_RELATIVE[i]], jnp.ones(codes.shape, jnp.float32))
        return contract_rows(chosen.astype(jnp.bfloat16), gathered[:, :share]).astype(jnp.bfloat16)

    def weigh(i, gathered):
        extra = gathered[:, share:].astype(jnp.float32)
        codes = extra[:, :top_count].astype(jnp.int32)
        scores = sum(extra[:, j * top_count : (j + 1) * top_count] for j in (1, 2, 3))
        factor = hit_sums(codes, groups, columns[BACK_RELATIVE[i]], scores)
        return jnp.concatenate(three_parts(factor), axis=0).astype(jnp.bfloat16)

    def own_hidden(slot_rows, pieces):
        summed, rest = first_stage(slot_rows, w_gate[0], w_up[0], pieces and (pieces[1], pieces[-1]))
        if pieces:
            summed = phase(*summed, pieces[2])[:2]
        gate, up = second_stage(summed, rest)
        return (jax.nn.silu(gate) * up).astype(jnp.bfloat16)

    def finish(pieces):
        return project(joined(pieces), w_down[0]).astype(jnp.bfloat16)

    def weighted(weights, returned):
        sums = project(weights, returned).reshape(3, sources, tok_rows, share)
        return (sums[0] + sums[1] + sums[2]).astype(jnp.bfloat16)

    def leave(partial):
        return exchange(partial, ("z", "y"))

    def total(collected):
        summed = jnp.sum(collected.reshape(n_z, n_rows, tok_rows, share).astype(jnp.float32), axis=0)
        return summed.astype(jnp.bfloat16).transpose(1, 0, 2).reshape(tok_rows, n_rows * share)

    gathered = [arrive(0), None]
    slots = plane_send(pick(0, gathered[0]), SEND_RELATIVE[0])
    gathered[1] = arrive(1)
    slots, gathered[1] = phase(slots, gathered[1])
    slots, rows = phase(slots, pick(1, gathered[1]))
    own = own_hidden(slots, None)
    slots = plane_send(rows, SEND_RELATIVE[1])
    weights = [weigh(i, gathered[i]) for i in range(steps)]
    own, slots = phase(own, slots)
    pieces = ring_gather(own, "y")
    returned = plane_return(finish(pieces), BACK_RELATIVE[0])
    result = finish(ring_gather(own_hidden(slots, pieces), "y"))
    blocks = plane_return(result, BACK_RELATIVE[1])
    partial = weighted(weights[0], returned)
    partial = phase(partial, blocks[1])[0]
    collected = leave(partial)
    returned = jnp.concatenate(blocks, axis=0)
    collected, returned = phase(collected, returned)
    last = leave(weighted(weights[1], returned))
    return jnp.stack([total(collected), total(last)])


def solution(mesh):
    split = Mesh(mesh.devices.reshape(8, 4, 2, 4), AXES)
    expert = ("z", "x", "c")
    return jax.shard_map(
        on_device,
        mesh=split,
        in_specs=(
            P(None, AXES, None),
            P(None, AXES, None),
            P(None, AXES, None),
            P(expert, "y", None),
            P(expert, "y", None),
            P(expert, None, "y"),
        ),
        out_specs=P(None, AXES, None),
        check_vma=False,
    )
```

```python
import jax
import jax.numpy as jnp
from jax import lax
from jax.sharding import Mesh, PartitionSpec as P

AXES = ("z", "x", "c", "y")
EXTRA = 128


def phase(*values):
    return lax.optimization_barrier(values)


def exchange(blocks, axes):
    return lax.all_to_all(blocks, axes, split_axis=0, concat_axis=0, tiled=True)


def shift(value, axis, by):
    n = lax.axis_size(axis)
    return lax.ppermute(value, axis, [(i, (i + by) % n) for i in range(n)])


def ring_gather(rows, axis):
    n = lax.axis_size(axis)
    blocks = {0: rows}
    upward = downward = rows
    for hop in range(1, (n + 1) // 2):
        upward, downward = shift(upward, axis, 1), shift(downward, axis, -1)
        blocks[n - hop], blocks[hop] = upward, downward
    half = -(-rows.shape[1] // 256) * 128
    blocks[n // 2] = jnp.concatenate(
        [shift(upward[:, :half], axis, 1), shift(downward[:, half:], axis, -1)], axis=1
    )
    return [blocks[i] for i in range(n)]


SEND_RELATIVE = (True, False)
BACK_RELATIVE = (False, True)
PEERS = ((0, 0), (0, 1), (2, 0), (2, 1), (1, 0), (1, 1), (3, 0), (3, 1))


def plane_shifts(blocks, sign):
    n_x, n_c = lax.axis_size("x"), lax.axis_size("c")
    moved = []
    for block, (step_x, step_c) in zip(blocks, PEERS):
        if step_x or step_c:
            pairs = [
                (x * n_c + c, (x + sign * step_x) % n_x * n_c + (c + step_c) % n_c)
                for x in range(n_x)
                for c in range(n_c)
            ]
            block = lax.ppermute(block, ("x", "c"), pairs)
        moved.append(block)
    return moved


def plane_places(sign):
    n_x, n_c = lax.axis_size("x"), lax.axis_size("c")
    x, c = lax.axis_index("x"), lax.axis_index("c")
    return [
        lax.rem(x + sign * step_x + n_x, n_x) * n_c + lax.rem(c + step_c, n_c) for step_x, step_c in PEERS
    ]


def plane_send(rows, relative):
    size = rows.shape[0] // len(PEERS)
    if not relative:
        return exchange(rows.reshape(len(PEERS), size, -1), ("x", "c")).reshape(rows.shape)
    moved = plane_shifts([rows[j * size : (j + 1) * size] for j in range(len(PEERS))], 1)
    arrived = jnp.zeros(rows.shape, rows.dtype)
    for block, place in zip(moved, plane_places(-1)):
        arrived = lax.dynamic_update_slice_in_dim(arrived, block, place * size, axis=0)
    return arrived


def plane_return(rows, relative):
    size = rows.shape[0] // len(PEERS)
    if not relative:
        return exchange(rows.reshape(len(PEERS), size, -1), ("x", "c")).reshape(rows.shape)
    blocks = [lax.dynamic_slice_in_dim(rows, place * size, size, axis=0) for place in plane_places(-1)]
    return plane_shifts(blocks, -1)


def slot_codes(owners, capacity):
    tok_rows = owners.shape[0]
    same = jnp.any(owners[:, :, None, None] == owners[None, None, :, :], axis=3)
    before = jnp.arange(tok_rows)[None, None, :] < jnp.arange(tok_rows)[:, None, None]
    return owners * capacity + jnp.sum((same & before).astype(jnp.int32), axis=2)


def three_parts(values):
    high = lax.reduce_precision(values, 8, 7)
    middle = lax.reduce_precision(values - high, 8, 7)
    return high, middle, values - high - middle


def with_extra(inputs, owners, scores, capacity):
    n_rows = lax.axis_size("y")
    tok_rows, width = inputs.shape
    shares = inputs.reshape(tok_rows, n_rows, width // n_rows).transpose(1, 0, 2)
    columns = [slot_codes(owners, capacity).astype(jnp.float32), *three_parts(scores)]
    extra = jnp.concatenate(columns, axis=1).astype(jnp.bfloat16)
    extra = jnp.pad(extra, ((0, 0), (0, EXTRA - extra.shape[1])))
    return jnp.concatenate(
        [shares, jnp.broadcast_to(extra[None], (n_rows, tok_rows, EXTRA))], axis=2
    )


def hit_sums(codes, groups, columns, values):
    keys = codes + groups[:, None]
    total = 0.0
    for k in range(codes.shape[1]):
        total = total + jnp.where(keys[:, k : k + 1] == columns[None, :], values[:, k : k + 1], 0.0)
    return total


def project(rows, weight):
    return jnp.dot(rows, weight, preferred_element_type=jnp.float32)


def contract_rows(left, right):
    return lax.dot_general(left, right, (((0,), (0,)), ((), ())), preferred_element_type=jnp.float32)


def block_rows(rows, offset):
    n = lax.axis_size("y")
    block = rows.shape[0] // n
    return lax.dynamic_slice_in_dim(rows, lax.rem(lax.axis_index("y") + offset, n) * block, block, axis=0)


def first_stage(slot_rows, wg, wu):
    block = slot_rows.shape[0] // lax.axis_size("y")
    far = block_rows(slot_rows, 2)
    far_gate, far_up = project(far, wg).astype(jnp.bfloat16), project(far, wu).astype(jnp.bfloat16)
    far_gate, far_up = shift(far_gate, "y", 1), shift(far_up, "y", -1)
    near = jnp.concatenate([block_rows(slot_rows, 1), block_rows(slot_rows, 3), block_rows(slot_rows, 0)], axis=0)
    gate, up = project(near, wg), project(near, wu)
    gate_next = (gate[:block] + far_gate.astype(jnp.float32)).astype(jnp.bfloat16)
    up_next = up[:block].astype(jnp.bfloat16)
    gate_prev = gate[block : 2 * block].astype(jnp.bfloat16)
    up_prev = (up[block : 2 * block] + far_up.astype(jnp.float32)).astype(jnp.bfloat16)
    return (gate_next, up_prev), (up_next, gate_prev, gate[2 * block :], up[2 * block :])


def second_stage(summed, rest):
    (gate_next, up_prev), (up_next, gate_prev, gate, up) = summed, rest
    for value, by in ((gate_next, 1), (gate_prev, -1)):
        gate = gate + shift(value, "y", by).astype(jnp.float32)
    for value, by in ((up_next, 1), (up_prev, -1)):
        up = up + shift(value, "y", by).astype(jnp.float32)
    return gate, up


def joined(pieces):
    n, block = len(pieces), pieces[0].shape[0]
    rows = jnp.zeros((n * block, pieces[0].shape[1]), pieces[0].dtype)
    for offset, piece in enumerate(pieces):
        start = lax.rem(lax.axis_index("y") + offset, n) * block
        rows = lax.dynamic_update_slice_in_dim(rows, piece, start, axis=0)
    return rows


def on_device(tokens, expert_ids, gate_scores, w_gate, w_up, w_down):
    steps, tok_rows, top_count = expert_ids.shape
    n_z, n_rows = lax.axis_size("z"), lax.axis_size("y")
    n_plane = lax.axis_size("x") * lax.axis_size("c")
    n_owner = n_z * n_plane
    share = tokens.shape[2] // n_rows
    capacity = max(2, min(tok_rows, 2 * tok_rows * top_count // n_owner))
    plane = lax.axis_index("z")
    span = n_owner * capacity
    sources = n_z * n_rows

    slot = jnp.arange(n_plane * sources * capacity, dtype=jnp.int32)
    index, source = slot // (sources * capacity), slot // capacity % sources
    size = sources * capacity
    relative = jnp.concatenate([jnp.full((size,), place, jnp.int32) for place in plane_places(1)])
    within = plane * n_plane * capacity + slot % capacity + span * source
    columns = {False: within + index * capacity, True: within + relative * capacity}
    tok = jnp.arange(sources * tok_rows, dtype=jnp.int32)
    groups = tok // tok_rows * span

    def arrive(i):
        packed = with_extra(tokens[i], expert_ids[i], gate_scores[i], capacity)
        return exchange(jnp.tile(packed, (n_z, 1, 1)), ("z", "y")).reshape(tok.shape[0], share + EXTRA)

    def pick(i, gathered):
        codes = gathered[:, share : share + top_count].astype(jnp.int32)
        chosen = hit_sums(codes, groups, columns[SEND_RELATIVE[i]], jnp.ones(codes.shape, jnp.float32))
        return contract_rows(chosen.astype(jnp.bfloat16), gathered[:, :share]).astype(jnp.bfloat16)

    def weigh(i, gathered):
        extra = gathered[:, share:].astype(jnp.float32)
        codes = extra[:, :top_count].astype(jnp.int32)
        scores = sum(extra[:, j * top_count : (j + 1) * top_count] for j in (1, 2, 3))
        factor = hit_sums(codes, groups, columns[BACK_RELATIVE[i]], scores)
        return jnp.concatenate(three_parts(factor), axis=0).astype(jnp.bfloat16)

    def own_hidden(slot_rows):
        gate, up = second_stage(*first_stage(slot_rows, w_gate[0], w_up[0]))
        return (jax.nn.silu(gate) * up).astype(jnp.bfloat16)

    def finish(pieces):
        return project(joined(pieces), w_down[0]).astype(jnp.bfloat16)

    def weighted(weights, returned):
        sums = project(weights, returned).reshape(3, sources, tok_rows, share)
        return (sums[0] + sums[1] + sums[2]).astype(jnp.bfloat16)

    def leave(partial):
        return exchange(partial, ("z", "y"))

    def total(collected):
        summed = jnp.sum(collected.reshape(n_z, n_rows, tok_rows, share).astype(jnp.float32), axis=0)
        return summed.astype(jnp.bfloat16).transpose(1, 0, 2).reshape(tok_rows, n_rows * share)

    gathered = [arrive(0), None]
    slots = plane_send(pick(0, gathered[0]), SEND_RELATIVE[0])
    gathered[1] = arrive(1)
    slots, gathered[1] = phase(slots, gathered[1])
    slots, rows = phase(slots, pick(1, gathered[1]))
    own = own_hidden(slots)
    slots = plane_send(rows, SEND_RELATIVE[1])
    weights = [weigh(i, gathered[i]) for i in range(steps)]
    own, slots = phase(own, slots)
    pieces = ring_gather(own, "y")
    returned = plane_return(finish(pieces), BACK_RELATIVE[0])
    result = finish(ring_gather(own_hidden(slots), "y"))
    blocks = plane_return(result, BACK_RELATIVE[1])
    partial = weighted(weights[0], returned)
    partial = phase(partial, blocks[1])[0]
    collected = leave(partial)
    returned = jnp.concatenate(blocks, axis=0)
    collected, returned = phase(collected, returned)
    last = leave(weighted(weights[1], returned))
    return jnp.stack([total(collected), total(last)])


def solution(mesh):
    split = Mesh(mesh.devices.reshape(8, 4, 2, 4), AXES)
    expert = ("z", "x", "c")
    return jax.shard_map(
        on_device,
        mesh=split,
        in_specs=(
            P(None, AXES, None),
            P(None, AXES, None),
            P(None, AXES, None),
            P(expert, "y", None),
            P(expert, "y", None),
            P(expert, None, "y"),
        ),
        out_specs=P(None, AXES, None),
        check_vma=False,
    )
```
